256 devices in a mesh: ctx: 64 (over x, z, y_hi), tp: 4 (over y_lo, core).
Axes of the slice: x: 4, y: 4 (y_hi: 2, y_lo: 2; y = y_hi * 2 + y_lo), z: 8, core: 2. Of those that a mesh axis runs over, the one named last changes fastest.
Arguments:
- trace_q: bfloat16 [8192, 5120], P(('ctx', 'tp')), may hold values from -120 to 120
- trace_key_value: bfloat16 [8192, 2048], P(('ctx', 'tp')), may hold values from -6 to 6
- suffix_q: bfloat16 [64, 128, 5120], P('ctx', 'tp'), may hold values from -120 to 120
- suffix_key_value: bfloat16 [64, 128, 2048], P('ctx', 'tp'), may hold values from -6 to 6
- prefix_len: int32 [64], P('ctx'), may hold values from 2048 to 8192, as said below
- del_start: int32 [64], P('ctx'), may hold values from 0 to 8191, as said below
- del_end: int32 [64], P('ctx'), may hold values from 1 to 8192, as said below
Outputs:
- trace_out: bfloat16 [8192, 5120], P(('ctx', 'tp'))
- suffix_out: bfloat16 [64, 128, 5120], P('ctx', 'tp')
The draws below stay inside these ranges and needn't reach their ends.
Inputs may be any that keep to these rules, and one draw needn't show every extreme that they name: `prefix_len`: one variant keeps the whole trace as prefix and deletes only its last position. del_start < prefix_len of the same variant. del_start < del_end <= prefix_len of the same variant, and del_end - del_start <= 1024.
All inputs are finite; a program needn't handle non-finite values.
Results may differ from the reference program's by a relative error of at most 0.0075.
Values may be sent and summed in bfloat16 or wider, within the bound.
A program may use at most 192 MiB of HBM per device.

```python
import jax
import jax.numpy as jnp
from jax import lax

QUERY_HEADS = 40
KEY_VALUE_HEADS = 8
HEAD_SIZE = 128
TOK_DEV = 128
SUFFIX_LENGTH = 128
TRACE_LENGTH = 8192
VARIANT_COUNT = 64
N_CTX = 64


def bounded_normal_draw(key, shape):
    return jnp.clip(jax.random.normal(key, shape, jnp.float32), -6.0, 6.0)


def drawn_queries(key, shape, salt):
    query_matrix = bounded_normal_draw(jax.random.fold_in(key, salt), shape)
    return query_matrix


def value_portion(key, shape, salt):
    return bounded_normal_draw(jax.random.fold_in(key, salt), shape)


def starting_trace_keys(key):
    return bounded_normal_draw(jax.random.fold_in(key, 101), (TRACE_LENGTH, KEY_VALUE_HEADS, HEAD_SIZE))


def starting_suffix_keys(key):
    return bounded_normal_draw(jax.random.fold_in(key, 111), (VARIANT_COUNT, SUFFIX_LENGTH, KEY_VALUE_HEADS, HEAD_SIZE))


def draw_trace_key_value(key, part):
    stacked_pairs = jnp.stack([starting_trace_keys(key), value_portion(key, (TRACE_LENGTH, KEY_VALUE_HEADS, HEAD_SIZE), 102)], axis=2)
    return stacked_pairs.reshape(TRACE_LENGTH, KEY_VALUE_HEADS * 2 * HEAD_SIZE).astype(jnp.bfloat16)


def draw_trace_q(key, part):
    query_matrix = drawn_queries(key, (TRACE_LENGTH, QUERY_HEADS, HEAD_SIZE), 103)
    return query_matrix.reshape(TRACE_LENGTH, QUERY_HEADS * HEAD_SIZE).astype(jnp.bfloat16)


def draw_suffix_key_value(key, part):
    stacked_pairs = jnp.stack([starting_suffix_keys(key), value_portion(key, (VARIANT_COUNT, SUFFIX_LENGTH, KEY_VALUE_HEADS, HEAD_SIZE), 112)], axis=3)
    return stacked_pairs.reshape(VARIANT_COUNT, SUFFIX_LENGTH, KEY_VALUE_HEADS * 2 * HEAD_SIZE).astype(jnp.bfloat16)


def draw_suffix_q(key, part):
    query_matrix = drawn_queries(key, (VARIANT_COUNT, SUFFIX_LENGTH, QUERY_HEADS, HEAD_SIZE), 113)
    return query_matrix.reshape(VARIANT_COUNT, SUFFIX_LENGTH, QUERY_HEADS * HEAD_SIZE).astype(jnp.bfloat16)


def deletion_spans(key):
    prefix = jax.random.randint(jax.random.fold_in(key, 201), (VARIANT_COUNT,), TRACE_LENGTH // 4, TRACE_LENGTH + 1)
    chosen_row = jax.random.randint(jax.random.fold_in(key, 202), (), 0, VARIANT_COUNT)
    is_chosen = jnp.arange(VARIANT_COUNT) == chosen_row
    prefix = jnp.where(is_chosen, TRACE_LENGTH, prefix).astype(jnp.int32)
    first = jax.random.randint(jax.random.fold_in(key, 203), (VARIANT_COUNT,), 0, prefix)
    span_size = jax.random.randint(jax.random.fold_in(key, 204), (VARIANT_COUNT,), 1, TRACE_LENGTH // 8 + 1)
    last = jnp.minimum(first + span_size, prefix)
    first = jnp.where(is_chosen, TRACE_LENGTH - 1, first)
    last = jnp.where(is_chosen, TRACE_LENGTH, last)
    return (prefix.astype(jnp.int32), first.astype(jnp.int32), last.astype(jnp.int32))


def draw_prefix_len(key, part):
    return deletion_spans(key)[0]


def draw_del_start(key, part):
    return deletion_spans(key)[1]


def draw_del_end(key, part):
    return deletion_spans(key)[2]


def setup_inputs(seed: int = 0) -> dict:
    arg_keys = jax.random.split(jax.random.key(seed), 8)
    return {
        "trace_q": draw_trace_q(jax.random.fold_in(arg_keys[7], 71), 0),
        "trace_key_value": draw_trace_key_value(jax.random.fold_in(arg_keys[7], 71), 0),
        "suffix_q": draw_suffix_q(jax.random.fold_in(arg_keys[7], 71), 0),
        "suffix_key_value": draw_suffix_key_value(jax.random.fold_in(arg_keys[7], 71), 0),
        "prefix_len": draw_prefix_len(jax.random.fold_in(arg_keys[7], 71), 0),
        "del_start": draw_del_start(jax.random.fold_in(arg_keys[7], 71), 0),
        "del_end": draw_del_end(jax.random.fold_in(arg_keys[7], 71), 0),
    }


def attend(query_matrix, key_rows, value_rows, allowed):
    element_count = query_matrix.shape[0]
    queries_per_group = QUERY_HEADS // KEY_VALUE_HEADS
    query_groups = query_matrix.reshape(element_count, KEY_VALUE_HEADS, queries_per_group, HEAD_SIZE).astype(jnp.float32)
    scores = jnp.einsum("qgjd,kgd->qgjk", query_groups, key_rows.astype(jnp.float32)) * (HEAD_SIZE ** -0.5)
    visible = allowed[:, None, None, :]
    largest = jnp.max(jnp.where(visible, scores, -1e30), axis=-1, keepdims=True)
    weights = jnp.where(visible, jnp.exp(scores - largest), 0.0)
    denominator = jnp.sum(weights, axis=-1)
    rounded = lax.optimization_barrier(weights.astype(jnp.bfloat16)).astype(jnp.float32)
    summed = jnp.einsum("qgjk,kgd->qgjd", rounded, value_rows.astype(jnp.float32))
    result = summed / denominator[..., None]
    return result.reshape(element_count, QUERY_HEADS * HEAD_SIZE).astype(jnp.bfloat16)


def reference(trace_q, trace_key_value, suffix_q, suffix_key_value, prefix_len, del_start, del_end):
    key_value_pairs = trace_key_value.reshape(TRACE_LENGTH, KEY_VALUE_HEADS, 2, HEAD_SIZE)
    trace_keys = key_value_pairs[:, :, 0]
    trace_values = key_value_pairs[:, :, 1]
    positions = jnp.arange(TRACE_LENGTH, dtype=jnp.int32)
    blocks = trace_q.reshape(N_CTX, TOK_DEV, QUERY_HEADS * HEAD_SIZE)

    def one_block(inputs):
        block_queries, number = inputs
        query_pos = number * TOK_DEV + jnp.arange(TOK_DEV, dtype=jnp.int32)
        allowed = positions[None, :] <= query_pos[:, None]
        return attend(block_queries, trace_keys, trace_values, allowed)

    trace_out = lax.map(one_block, (blocks, jnp.arange(N_CTX, dtype=jnp.int32))).reshape(TRACE_LENGTH, QUERY_HEADS * HEAD_SIZE)
    suffix_key_value_pairs = suffix_key_value.reshape(VARIANT_COUNT, SUFFIX_LENGTH, KEY_VALUE_HEADS, 2, HEAD_SIZE)
    own_rows = jnp.arange(SUFFIX_LENGTH, dtype=jnp.int32)

    def one_variant(inputs):
        query_matrix, variant_pairs, prefix, first, last = inputs
        key_rows = jnp.concatenate([trace_keys, variant_pairs[:, :, 0]], axis=0)
        value_rows = jnp.concatenate([trace_values, variant_pairs[:, :, 1]], axis=0)
        kept = (positions < prefix) & ((positions < first) | (positions >= last))
        prefix_ok = jnp.broadcast_to(kept[None, :], (SUFFIX_LENGTH, TRACE_LENGTH))
        self_ok = own_rows[None, :] <= own_rows[:, None]
        allowed = jnp.concatenate([prefix_ok, self_ok], axis=1)
        return attend(query_matrix, key_rows, value_rows, allowed)

    suffix_out = lax.map(one_variant, (suffix_q, suffix_key_value_pairs, prefix_len, del_start, del_end))
    return trace_out, suffix_out
```

```python
import math

import jax
import jax.numpy as jnp
from jax import lax
from jax.experimental import pallas as pl
from jax.experimental.pallas import tpu as pltpu
from jax.sharding import PartitionSpec as P

HEAD = 128
GROUP = 5
ROWS = GROUP * 128
QCOL = GROUP * HEAD
SCALE = HEAD ** (-0.5) * math.log2(math.e)
LOW = -1e30
MESH = pl.DeviceIdType.MESH
LAG = 2


def dot(a, b, ca, cb):
    return lax.dot_general(a, b, (((ca,), (cb,)), ((), ())), preferred_element_type=jnp.float32)


def kernel(
    tq, tkv, sq, skv, pre, first, last,
    tout, sout,
    kvb, tqb, sqb, skb, tob, sob, meta_out, meta, acc, m, l,
    st_send, st_recv, meta_send, meta_recv, ag0, ag_send, ag_recv, o_send, o_recv,
):
    ctx = lax.axis_index("ctx")
    tp = lax.axis_index("tp")
    x = ctx // 16
    z = (ctx // 2) % 8
    yh = ctx % 2
    yl = tp // 2
    c = tp % 2
    u = x // 2
    p = ((x + 1) // 2) % 2
    pb = 1 - p
    cb = 1 - c
    head = u * 4 + yh * 2 + yl

    def xof(side, par):
        return par + side * (3 - 2 * par)

    def dev(side, par, zz, yyh, yyl, cc):
        return (xof(side, par) * 16 + zz * 2 + yyh, yyl * 2 + cc)

    def flip(a, by):
        return 1 - a if by else a

    home = (yh + u) % 2
    at_home = c == home
    spot = yl * 2 + c

    up = dev(u, p, (z + 1) % 8, yh, yl, c)
    down = dev(u, p, (z + 7) % 8, yh, yl, c)
    across = dev(u, pb, z, yh, yl, c)
    sibling = dev(u, p, z, yh, yl, cb)

    barrier = pltpu.get_barrier_semaphore()
    for i in range(1, 16):
        pl.semaphore_signal(
            barrier, inc=1, device_id_type=MESH,
            device_id=dev(flip(u, i // 8), p, z, flip(yh, i // 4 % 2), flip(yl, i // 2 % 2), flip(c, i % 2)),
        )
    for d in (up, down, across):
        pl.semaphore_signal(barrier, inc=1, device_id=d, device_id_type=MESH)
    pl.semaphore_wait(barrier, 18)

    def block(par, zz, cc, s):
        xx = par if s == 0 else 3 - par
        return zz * 8 + xx * 2 + (cc + s) % 2

    def rows(b):
        return kvb.at[pl.ds(pl.multiple_of(b * 128, 128), 128), :]

    mine = pl.ds(pl.multiple_of(spot * 32, 32), 32)
    here = pl.ds(pl.multiple_of((z * 8 + x * 2 + yh) * 128 + spot * 32, 32), 32)

    def targets(kind, i):
        h2 = flip(u, i // 4) * 4 + flip(yh, i // 2 % 2) * 2 + flip(yl, i % 2)
        to = dev(flip(u, i // 4), p, z, flip(yh, i // 2 % 2), flip(yl, i % 2), home)
        wide = pl.ds(pl.multiple_of(h2 * QCOL, 128), QCOL)
        pair = pl.ds(pl.multiple_of(h2 * 256, 128), 256)
        src, dst = (
            (tkv.at[:, pair], kvb.at[here, :]),
            (tq.at[:, wide], tqb.at[u, mine, :]),
            (skv.at[:, pair], skb.at[u, mine, :]),
            (sq.at[:, wide], sqb.at[u, mine, :]),
        )[kind]
        remote = pltpu.make_async_remote_copy(
            src, dst, st_send.at[kind, i], st_recv.at[kind, u], device_id=to, device_id_type=MESH
        )
        local = pltpu.make_async_copy(src, dst, st_recv.at[kind, u])
        return remote, local

    def stage_start(kind):
        for i in range(7, -1, -1):
            remote, local = targets(kind, i)
            if i:
                remote.start()
            else:
                pl.when(at_home)(local.start)
                pl.when(jnp.logical_not(at_home))(remote.start)

    def stage_drain(kind):
        for i in range(7, -1, -1):
            remote, _ = targets(kind, i)
            if i:
                remote.wait_send()
            else:
                pl.when(jnp.logical_not(at_home))(remote.wait_send)

    def stage_arrive(kind, s):
        dst = (rows(block(p, z, c, s)), tqb.at[s], skb.at[s], sqb.at[s])[kind]
        pltpu.make_async_copy(dst, dst, st_recv.at[kind, s]).wait()

    def meta_copy(i):
        to = dev(flip(u, i), p, z, yl, c, home)
        is_self = jnp.logical_and(jnp.logical_and(yl == yh, c == yl), at_home) if i == 0 else None
        remote = pltpu.make_async_remote_copy(
            meta_out, meta.at[u], meta_send.at[i], meta_recv.at[u], device_id=to, device_id_type=MESH
        )
        local = pltpu.make_async_copy(meta_out, meta.at[u], meta_recv.at[u])
        return remote, local, is_self

    def pass_on(b, to, sem):
        return pltpu.make_async_remote_copy(rows(b), rows(b), sem, ag_recv.at[b], device_id=to, device_id_type=MESH)

    def arrive(b):
        pltpu.make_async_copy(rows(b), rows(b), ag_recv.at[b]).wait()

    def own_copies():
        a, b = block(p, z, c, 0), block(p, z, c, 1)
        return [
            pass_on(a, across, ag0.at[0]),
            pass_on(a, up, ag0.at[1]),
            pass_on(a, down, ag0.at[2]),
            pass_on(b, up, ag0.at[3]),
            pass_on(b, down, ag0.at[4]),
            pass_on(b, across, ag0.at[5]),
            pass_on(a, sibling, ag0.at[6]),
            pass_on(b, sibling, ag0.at[7]),
        ]

    def near_copies():
        a, b = block(pb, z, c, 0), block(pb, z, c, 1)
        return (
            [pass_on(a, up, ag0.at[8]), pass_on(a, down, ag0.at[9]), pass_on(a, sibling, ag0.at[10])],
            [pass_on(b, sibling, ag0.at[11])],
        )

    def zstep(j):
        return (z + 8 + (1 - 2 * (j % 2)) * ((j + 1) // 2)) % 8

    def ring_copies(j):
        zz = zstep(j)
        step = 2 * (j % 2) - 1
        onward = dev(u, p, (z + 8 + step) % 8, yh, yl, c)
        early = j <= 4
        go = (
            jnp.logical_or(early, j == 5),
            jnp.logical_or(early, j == 6),
            jnp.logical_or(early, j == 5 + c),
        )
        ids = (block(p, zz, c, 0), block(pb, zz, c, 0), block(p, zz, c, 1))
        return zz, go, ids, onward

    def ring(j):
        zz, go, ids, onward = ring_copies(j)
        for i in range(3):
            arrive(ids[i])
            pl.when(go[i])(pass_on(ids[i], onward, ag_send.at[j, i]).start)
            if i == 2:
                pass_on(ids[i], across, ag_send.at[j, 6]).start()
            pass_on(ids[i], sibling, ag_send.at[j, 3 + i]).start()

    def cross(j):
        b = block(pb, zstep(j), c, 1)
        arrive(b)
        pass_on(b, sibling, ag_send.at[j, 7]).start()

    def drain(j):
        zz, go, ids, onward = ring_copies(j)
        for i in range(3):
            pl.when(go[i])(pass_on(ids[i], onward, ag_send.at[j, i]).wait_send)
            pass_on(ids[i], sibling, ag_send.at[j, 3 + i]).wait_send()
        pass_on(ids[2], across, ag_send.at[j, 6]).wait_send()
        pass_on(block(pb, zz, c, 1), sibling, ag_send.at[j, 7]).wait_send()

    def from_sibling(j):
        zz = zstep(j)
        for par in (0, 1):
            for s in (0, 1):
                arrive(block(par, zz, cb, s))

    def queries(buf, s):
        return jnp.concatenate([buf[s, :, i * HEAD:(i + 1) * HEAD] for i in range(GROUP)], axis=0)

    def wide_of(a, n):
        return jnp.concatenate([a] * n, axis=1)

    def fold(q, s, v):
        n = s.shape[1] // 128
        before = m[q]
        top = s[:, :128]
        for t in range(1, n):
            top = jnp.maximum(top, s[:, t * 128:(t + 1) * 128])
        now = jnp.maximum(before, jnp.max(top, axis=1, keepdims=True) * SCALE)
        m[q] = now
        shrink = jnp.exp2(before - now)
        w = jnp.exp2(s * SCALE - wide_of(now, n))
        part = w[:, :128]
        for t in range(1, n):
            part = part + w[:, t * 128:(t + 1) * 128]
        acc[q] = acc[q] * shrink + dot(w.astype(jnp.bfloat16), v, 1, 0)
        l[q] = l[q] * shrink + part

    def trace_body(zz, par, reach):
        at = pl.multiple_of(zz * 1024, 1024)
        counts = [(par if s == 0 else 3 - par) + reach for s in (0, 1)]
        scores = []
        for s in (0, 1):
            n = counts[s]
            if n == 0:
                scores.append(None)
                continue
            sc = dot(queries(tqb, s), kvb[pl.ds(at, n * 256), :HEAD], 1, 1)
            if reach:
                row = lax.broadcasted_iota(jnp.int32, (ROWS, 256), 0) % 128
                lane = lax.broadcasted_iota(jnp.int32, (ROWS, 256), 1)
                seen = lane - row <= (z - zz) * 256 + ((c + s) % 2) * 128
                tail = jnp.where(seen, sc[:, (n - 1) * 256:], LOW)
                sc = tail if n == 1 else jnp.concatenate([sc[:, :(n - 1) * 256], tail], axis=1)
            scores.append(sc)
        for s in (0, 1):
            if scores[s] is not None:
                fold(s, scores[s], kvb[pl.ds(at, counts[s] * 256), HEAD:])

    def trace_step(j):
        zz = zstep(j)
        for par in (0, 1):
            for reach in (0, 1):
                fits = jnp.logical_and(p == par, zz <= z if reach else zz > z)
                pl.when(fits)(lambda par=par, reach=reach: trace_body(zz, par, reach))

    def suffix_self():
        for s in (0, 1):
            sc = dot(queries(sqb, s), skb[s, :, :HEAD], 1, 1)
            row = lax.broadcasted_iota(jnp.int32, (ROWS, 128), 0) % 128
            lane = lax.broadcasted_iota(jnp.int32, (ROWS, 128), 1)
            fold(2 + s, jnp.where(lane <= row, sc, LOW), skb[s, :, HEAD:])

    def suffix_step(j):
        zz = zstep(j)
        at = pl.multiple_of(zz * 1024, 1024)
        scores = []
        for s in (0, 1):
            sc = dot(queries(sqb, s), kvb[pl.ds(at, 1024), :HEAD], 1, 1)
            bias = []
            for t in range(8):
                pos = (t // 2) * 2048 + (t % 2) * 128 + zz * 256 + lax.broadcasted_iota(jnp.int32, (1, 128), 1)
                limit, lo, hi = meta[s, 0:1, :], meta[s, 1:2, :], meta[s, 2:3, :]
                seen = jnp.logical_and(pos < limit, jnp.logical_or(pos < lo, pos >= hi))
                bias.append(jnp.where(seen, 0.0, LOW))
            scores.append(sc + jnp.concatenate(bias, axis=1))
        for s in (0, 1):
            fold(2 + s, scores[s], kvb[pl.ds(at, 1024), HEAD:])

    def returns(kind, s, i):
        buf, out = ((tob, tout), (sob, sout))[kind]
        yyl, cc = flip(yl, i // 2), flip(c, i % 2)
        to = dev(s, p, z, (c + s) % 2, yyl, cc)
        part = pl.ds(pl.multiple_of((yyl * 2 + cc) * 32, 32), 32)
        place = pl.ds(pl.multiple_of(head * QCOL, 128), QCOL)
        remote = pltpu.make_async_remote_copy(
            buf.at[s, part, :], out.at[:, place], o_send.at[kind, s, i], o_recv.at[kind],
            device_id=to, device_id_type=MESH,
        )
        local = pltpu.make_async_copy(buf.at[s, part, :], out.at[:, place], o_recv.at[kind])
        is_self = jnp.logical_and(at_home, u == s) if i == 0 else None
        return remote, local, is_self

    def hand_back(kind):
        buf = (tob, sob)[kind]
        for s in (0, 1):
            q = kind * 2 + s
            res = (acc[q] / jnp.sum(l[q], axis=1, keepdims=True)).astype(jnp.bfloat16)
            for i in range(GROUP):
                buf[s, :, i * HEAD:(i + 1) * HEAD] = res[i * 128:(i + 1) * 128]
            for i in range(3, -1, -1):
                remote, local, is_self = returns(kind, s, i)
                if i:
                    remote.start()
                else:
                    pl.when(is_self)(local.start)
                    pl.when(jnp.logical_not(is_self))(remote.start)

    stage_start(0)
    meta_out[0:1, :] = jnp.full((1, 128), pre[0], jnp.int32)
    meta_out[1:2, :] = jnp.full((1, 128), first[0], jnp.int32)
    meta_out[2:8, :] = jnp.full((6, 128), last[0], jnp.int32)
    stage_start(1)
    for i in (0, 1):
        remote, local, is_self = meta_copy(i)
        if i:
            remote.start()
        else:
            pl.when(is_self)(local.start)
            pl.when(jnp.logical_not(is_self))(remote.start)

    acc[...] = jnp.zeros_like(acc)
    l[...] = jnp.zeros_like(l)
    m[...] = jnp.full_like(m, LOW)

    for s in (0, 1):
        stage_arrive(0, s)
    for copy in own_copies():
        copy.start()
    for s in (0, 1):
        stage_arrive(1, s)
    stage_start(2)
    stage_start(3)
    near_a, near_b = near_copies()
    arrive(block(pb, z, c, 0))
    for copy in near_a:
        copy.start()
    arrive(block(pb, z, c, 1))
    for copy in near_b:
        copy.start()
    ring(1)

    def step(k, _):
        @pl.when(k < 8)
        def _():
            from_sibling(k)
            trace_step(k)

        pl.when(k < 6)(lambda: ring(k + 2))
        pl.when(k < 7)(lambda: cross(k + 1))

        pl.when(k == 7)(lambda: hand_back(0))

        @pl.when(k == LAG - 1)
        def _():
            for s in (0, 1):
                stage_arrive(2, s)
                stage_arrive(3, s)
                pltpu.make_async_copy(meta.at[s], meta.at[s], meta_recv.at[s]).wait()
            suffix_self()

        pl.when(k >= LAG)(lambda: suffix_step(k - LAG))
        return 0

    lax.fori_loop(0, 8 + LAG, step, 0)
    hand_back(1)

    for kind in range(4):
        stage_drain(kind)
    for i in (0, 1):
        remote, _, is_self = meta_copy(i)
        if i:
            remote.wait_send()
        else:
            pl.when(jnp.logical_not(is_self))(remote.wait_send)
    for copy in own_copies() + near_a + near_b:
        copy.wait_send()

    def finish(j, _):
        drain(j)
        return 0

    lax.fori_loop(1, 8, finish, 0)
    for kind in (0, 1):
        for s in (0, 1):
            for i in range(4):
                remote, _, is_self = returns(kind, s, i)
                if i:
                    remote.wait_send()
                else:
                    pl.when(jnp.logical_not(is_self))(remote.wait_send)
    pltpu.make_async_copy(tout, tout, o_recv.at[0]).wait()
    pltpu.make_async_copy(sout, sout, o_recv.at[1]).wait()


def local(trace_q, trace_key_value, suffix_q, suffix_key_value, prefix_len, del_start, del_end):
    any_space = pl.BlockSpec(memory_space=pl.ANY)
    scalar = pl.BlockSpec(memory_space=pltpu.SMEM)
    bf16, f32 = jnp.bfloat16, jnp.float32
    tout, sout = pl.pallas_call(
        kernel,
        out_shape=(
            jax.ShapeDtypeStruct(trace_q.shape, bf16),
            jax.ShapeDtypeStruct(trace_q.shape, bf16),
        ),
        in_specs=[any_space] * 4 + [scalar] * 3,
        out_specs=(any_space, any_space),
        scratch_shapes=[
            pltpu.VMEM((8192, 256), bf16),
            pltpu.VMEM((2, 128, QCOL), bf16),
            pltpu.VMEM((2, 128, QCOL), bf16),
            pltpu.VMEM((2, 128, 256), bf16),
            pltpu.VMEM((2, 128, QCOL), bf16),
            pltpu.VMEM((2, 128, QCOL), bf16),
            pltpu.VMEM((8, 128), jnp.int32),
            pltpu.VMEM((2, 8, 128), jnp.int32),
            pltpu.VMEM((4, ROWS, HEAD), f32),
            pltpu.VMEM((4, ROWS, HEAD), f32),
            pltpu.VMEM((4, ROWS, HEAD), f32),
            pltpu.SemaphoreType.DMA((4, 8)),
            pltpu.SemaphoreType.DMA((4, 2)),
            pltpu.SemaphoreType.DMA((2,)),
            pltpu.SemaphoreType.DMA((2,)),
            pltpu.SemaphoreType.DMA((12,)),
            pltpu.SemaphoreType.DMA((8, 8)),
            pltpu.SemaphoreType.DMA((64,)),
            pltpu.SemaphoreType.DMA((2, 2, 4)),
            pltpu.SemaphoreType.DMA((2,)),
        ],
        compiler_params=pltpu.CompilerParams(
            collective_id=0, has_side_effects=True, vmem_limit_bytes=56 * 2**20
        ),
        cost_estimate=pl.CostEstimate(flops=9 * 10**9, bytes_accessed=4 * 10**6, transcendentals=17 * 10**6),
    )(
        trace_q, trace_key_value, suffix_q[0], suffix_key_value[0], prefix_len, del_start, del_end
    )
    return tout, sout[None]


def solution(mesh):
    return jax.shard_map(
        local,
        mesh=mesh,
        in_specs=(
            P(("ctx", "tp"), None),
            P(("ctx", "tp"), None),
            P("ctx", "tp", None),
            P("ctx", "tp", None),
            P("ctx"),
            P("ctx"),
            P("ctx"),
        ),
        out_specs=(P(("ctx", "tp"), None), P("ctx", "tp", None)),
        check_vma=False,
    )
```

```python
import math

import jax
import jax.numpy as jnp
from jax import lax
from jax.experimental import pallas as pl
from jax.experimental.pallas import tpu as pltpu
from jax.sharding import PartitionSpec as P

HEAD = 128
GROUP = 5
ROWS = GROUP * 128
QCOL = GROUP * HEAD
SCALE = HEAD ** (-0.5) * math.log2(math.e)
LOW = -1e30
MESH = pl.DeviceIdType.MESH


def dot(a, b, ca, cb):
    return lax.dot_general(a, b, (((ca,), (cb,)), ((), ())), preferred_element_type=jnp.float32)


def kernel(
    tq, tkv, sq, skv, pre, first, last,
    tout, sout,
    kvb, tqb, sqb, skb, tob, sob, meta_out, meta, acc, m, l,
    st_send, st_recv, meta_send, meta_recv, ag0, ag_send, ag_recv, o_send, o_recv,
):
    ctx = lax.axis_index("ctx")
    tp = lax.axis_index("tp")
    x = ctx // 16
    z = (ctx // 2) % 8
    yh = ctx % 2
    yl = tp // 2
    c = tp % 2
    u = x // 2
    p = ((x + 1) // 2) % 2
    pb = 1 - p
    cb = 1 - c
    head = u * 4 + yh * 2 + yl

    def xof(side, par):
        return par + side * (3 - 2 * par)

    def dev(side, par, zz, yyh, yyl, cc):
        return (xof(side, par) * 16 + zz * 2 + yyh, yyl * 2 + cc)

    def flip(a, by):
        return 1 - a if by else a

    home = (yh + u) % 2
    at_home = c == home
    spot = yl * 2 + c

    up = dev(u, p, (z + 1) % 8, yh, yl, c)
    down = dev(u, p, (z + 7) % 8, yh, yl, c)
    across = dev(u, pb, z, yh, yl, c)
    sibling = dev(u, p, z, yh, yl, cb)

    barrier = pltpu.get_barrier_semaphore()
    for i in range(1, 32):
        pl.semaphore_signal(
            barrier, inc=1, device_id_type=MESH,
            device_id=dev(
                flip(u, i // 8 % 2), flip(p, i // 16), z, flip(yh, i // 4 % 2), flip(yl, i // 2 % 2), flip(c, i % 2)
            ),
        )
    for d in (up, down):
        pl.semaphore_signal(barrier, inc=1, device_id=d, device_id_type=MESH)
    pl.semaphore_wait(barrier, 33)

    def block(par, zz, cc, s):
        xx = par if s == 0 else 3 - par
        return zz * 8 + xx * 2 + (cc + s) % 2

    def rows(b):
        return kvb.at[pl.ds(pl.multiple_of(b * 128, 128), 128), :]

    mine = pl.ds(pl.multiple_of(spot * 32, 32), 32)
    here = pl.ds(pl.multiple_of((z * 8 + x * 2 + yh) * 128 + spot * 32, 32), 32)

    def targets(kind, i):
        h2 = flip(u, i // 4) * 4 + flip(yh, i // 2 % 2) * 2 + flip(yl, i % 2)
        to = dev(flip(u, i // 4), pb if kind == 4 else p, z, flip(yh, i // 2 % 2), flip(yl, i % 2), home)
        wide = pl.ds(pl.multiple_of(h2 * QCOL, 128), QCOL)
        pair = pl.ds(pl.multiple_of(h2 * 256, 128), 256)
        src, dst = (
            (tkv.at[:, pair], kvb.at[here, :]),
            (tq.at[:, wide], tqb.at[u, mine, :]),
            (skv.at[:, pair], skb.at[u, mine, :]),
            (sq.at[:, wide], sqb.at[u, mine, :]),
            (tkv.at[:, pair], kvb.at[here, :]),
        )[kind]
        remote = pltpu.make_async_remote_copy(
            src, dst, st_send.at[kind, i], st_recv.at[kind, u], device_id=to, device_id_type=MESH
        )
        local = pltpu.make_async_copy(src, dst, st_recv.at[kind, u])
        return remote, local

    def stage_start(kind):
        for i in range(7, -1, -1):
            remote, local = targets(kind, i)
            if i or kind == 4:
                remote.start()
            else:
                pl.when(at_home)(local.start)
                pl.when(jnp.logical_not(at_home))(remote.start)

    def stage_drain(kind):
        for i in range(7, -1, -1):
            remote, _ = targets(kind, i)
            if i or kind == 4:
                remote.wait_send()
            else:
                pl.when(jnp.logical_not(at_home))(remote.wait_send)

    def stage_arrive(kind, s):
        dst = (rows(block(p, z, c, s)), tqb.at[s], skb.at[s], sqb.at[s], rows(block(pb, z, c, s)))[kind]
        pltpu.make_async_copy(dst, dst, st_recv.at[kind, s]).wait()

    def meta_copy(i):
        to = dev(flip(u, i), p, z, yl, c, home)
        is_self = jnp.logical_and(jnp.logical_and(yl == yh, c == yl), at_home) if i == 0 else None
        remote = pltpu.make_async_remote_copy(
            meta_out, meta.at[u], meta_send.at[i], meta_recv.at[u], device_id=to, device_id_type=MESH
        )
        local = pltpu.make_async_copy(meta_out, meta.at[u], meta_recv.at[u])
        return remote, local, is_self

    def pass_on(b, to, sem):
        return pltpu.make_async_remote_copy(rows(b), rows(b), sem, ag_recv.at[b], device_id=to, device_id_type=MESH)

    def arrive(b):
        pltpu.make_async_copy(rows(b), rows(b), ag_recv.at[b]).wait()

    def own_copies():
        a, b = block(p, z, c, 0), block(p, z, c, 1)
        return [
            pass_on(b, up, ag0.at[0]),
            pass_on(b, down, ag0.at[1]),
            pass_on(b, across, ag0.at[2]),
            pass_on(a, up, ag0.at[3]),
            pass_on(a, down, ag0.at[4]),
            pass_on(b, sibling, ag0.at[5]),
            pass_on(a, sibling, ag0.at[6]),
        ]

    def near_copies():
        a, b = block(pb, z, c, 0), block(pb, z, c, 1)
        return (
            [pass_on(a, up, ag0.at[7]), pass_on(a, down, ag0.at[8]), pass_on(a, sibling, ag0.at[9])],
            [pass_on(b, sibling, ag0.at[10])],
        )

    def zstep(j):
        return (z + 8 + (1 - 2 * (j % 2)) * ((j + 1) // 2)) % 8

    def ring_copies(j):
        zz = zstep(j)
        step = 2 * (j % 2) - 1
        onward = dev(u, p, (z + 8 + step) % 8, yh, yl, c)
        early = j <= 4
        go = (
            jnp.logical_or(early, j == 5),
            jnp.logical_or(early, j == 6),
            jnp.logical_or(early, j == 5 + c),
        )
        ids = (block(p, zz, c, 0), block(pb, zz, c, 0), block(p, zz, c, 1))
        return zz, go, ids, onward

    def ring(j, which):
        zz, go, ids, onward = ring_copies(j)
        for i in which:
            arrive(ids[i])
            pl.when(go[i])(pass_on(ids[i], onward, ag_send.at[j, i]).start)
            if i == 2:
                pass_on(ids[i], across, ag_send.at[j, 6]).start()
            pass_on(ids[i], sibling, ag_send.at[j, 3 + i]).start()

    def cross(j):
        b = block(pb, zstep(j), c, 1)
        arrive(b)
        pass_on(b, sibling, ag_send.at[j, 7]).start()

    def drain(j):
        zz, go, ids, onward = ring_copies(j)
        for i in range(3):
            pl.when(go[i])(pass_on(ids[i], onward, ag_send.at[j, i]).wait_send)
            pass_on(ids[i], sibling, ag_send.at[j, 3 + i]).wait_send()
        pass_on(ids[2], across, ag_send.at[j, 6]).wait_send()
        pass_on(block(pb, zz, c, 1), sibling, ag_send.at[j, 7]).wait_send()

    def from_sibling(j):
        zz = zstep(j)
        for par in (0, 1):
            for s in (0, 1):
                arrive(block(par, zz, cb, s))

    def queries(buf, s):
        return jnp.concatenate([buf[s, :, i * HEAD:(i + 1) * HEAD] for i in range(GROUP)], axis=0)

    def wide_of(a, n):
        return jnp.concatenate([a] * n, axis=1)

    def fold(q, pieces, r=slice(0, ROWS)):
        before = m[q, r]
        cols = [sc[:, t * 128:(t + 1) * 128] for sc, _ in pieces for t in range(sc.shape[1] // 128)]
        top = cols[0]
        for col in cols[1:]:
            top = jnp.maximum(top, col)
        now = jnp.maximum(before, jnp.max(top, axis=1, keepdims=True) * SCALE)
        m[q, r] = now
        shrink = jnp.exp2(before - now)
        total, part = acc[q, r] * shrink, l[q, r] * shrink
        for sc, v in pieces:
            n = sc.shape[1] // 128
            w = jnp.exp2(sc * SCALE - wide_of(now, n))
            for t in range(n):
                part = part + w[:, t * 128:(t + 1) * 128]
            total = total + dot(w.astype(jnp.bfloat16), v, 1, 0)
        acc[q, r] = total
        l[q, r] = part

    def trace_body(zz, par, reach):
        at = pl.multiple_of(zz * 1024, 1024)
        counts = [(par if s == 0 else 3 - par) + reach for s in (0, 1)]
        scores = []
        for s in (0, 1):
            n = counts[s]
            if n == 0:
                scores.append(None)
                continue
            sc = dot(queries(tqb, s), kvb[pl.ds(at, n * 256), :HEAD], 1, 1)
            if reach:
                row = lax.broadcasted_iota(jnp.int32, (ROWS, 256), 0) % 128
                lane = lax.broadcasted_iota(jnp.int32, (ROWS, 256), 1)
                seen = lane - row <= (z - zz) * 256 + ((c + s) % 2) * 128
                tail = jnp.where(seen, sc[:, (n - 1) * 256:], LOW)
                sc = tail if n == 1 else jnp.concatenate([sc[:, :(n - 1) * 256], tail], axis=1)
            scores.append(sc)
        for s in (0, 1):
            if scores[s] is not None:
                fold(s, [(scores[s], kvb[pl.ds(at, counts[s] * 256), HEAD:])])

    def trace_step(j):
        zz = zstep(j)
        for par in (0, 1):
            for reach in (0, 1):
                fits = jnp.logical_and(p == par, zz <= z if reach else zz > z)
                pl.when(fits)(lambda par=par, reach=reach: trace_body(zz, par, reach))

    def suffix_self():
        for s in (0, 1):
            sc = dot(queries(sqb, s), skb[s, :, :HEAD], 1, 1)
            row = lax.broadcasted_iota(jnp.int32, (ROWS, 128), 0) % 128
            lane = lax.broadcasted_iota(jnp.int32, (ROWS, 128), 1)
            fold(2 + s, [(jnp.where(lane <= row, sc, LOW), skb[s, :, HEAD:])])

    def suffix_step(s, planes):
        q = queries(sqb, s)
        limit, lo, hi = meta[s, 0:1, :], meta[s, 1:2, :], meta[s, 2:3, :]
        biases = []
        for zz in planes:
            bias = []
            for t in range(8):
                pos = (t // 2) * 2048 + (t % 2) * 128 + zz * 256 + lax.broadcasted_iota(jnp.int32, (1, 128), 1)
                seen = jnp.logical_and(pos < limit, jnp.logical_or(pos < lo, pos >= hi))
                bias.append(jnp.where(seen, 0.0, LOW))
            biases.append(jnp.concatenate(bias, axis=1))
        halves = (slice(0, ROWS // 2), slice(ROWS // 2, ROWS))
        places = [pl.ds(pl.multiple_of(zz * 1024, 1024), 1024) for zz in planes]
        scores = [
            [dot(q[r], kvb[at, :HEAD], 1, 1) + bias for at, bias in zip(places, biases)] for r in halves
        ]
        for r, row in zip(halves, scores):
            fold(2 + s, [(sc, kvb[at, HEAD:]) for sc, at in zip(row, places)], r)

    def returns(kind, s, i):
        buf, out = ((tob, tout), (sob, sout))[kind]
        yyl, cc = flip(yl, i // 2), flip(c, i % 2)
        to = dev(s, p, z, (c + s) % 2, yyl, cc)
        part = pl.ds(pl.multiple_of((yyl * 2 + cc) * 32, 32), 32)
        place = pl.ds(pl.multiple_of(head * QCOL, 128), QCOL)
        remote = pltpu.make_async_remote_copy(
            buf.at[s, part, :], out.at[:, place], o_send.at[kind, s, i], o_recv.at[kind],
            device_id=to, device_id_type=MESH,
        )
        local = pltpu.make_async_copy(buf.at[s, part, :], out.at[:, place], o_recv.at[kind])
        is_self = jnp.logical_and(at_home, u == s) if i == 0 else None
        return remote, local, is_self

    def hand_back(kind, slots):
        buf = (tob, sob)[kind]
        for s in slots:
            q = kind * 2 + s
            res = (acc[q] / jnp.sum(l[q], axis=1, keepdims=True)).astype(jnp.bfloat16)
            for i in range(GROUP):
                buf[s, :, i * HEAD:(i + 1) * HEAD] = res[i * 128:(i + 1) * 128]
            for i in range(3, -1, -1):
                remote, local, is_self = returns(kind, s, i)
                if i:
                    remote.start()
                else:
                    pl.when(is_self)(local.start)
                    pl.when(jnp.logical_not(is_self))(remote.start)

    stage_start(0)
    pl.when(u == 0)(lambda: stage_start(4))
    meta_out[0:1, :] = jnp.full((1, 128), pre[0], jnp.int32)
    meta_out[1:2, :] = jnp.full((1, 128), first[0], jnp.int32)
    meta_out[2:8, :] = jnp.full((6, 128), last[0], jnp.int32)
    stage_start(1)
    for i in (0, 1):
        remote, local, is_self = meta_copy(i)
        if i:
            remote.start()
        else:
            pl.when(is_self)(local.start)
            pl.when(jnp.logical_not(is_self))(remote.start)

    acc[...] = jnp.zeros_like(acc)
    l[...] = jnp.zeros_like(l)
    m[...] = jnp.full_like(m, LOW)

    for s in (0, 1):
        stage_arrive(0, s)
    for copy in own_copies():
        copy.start()
    stage_start(3)
    stage_start(2)
    near_a, near_b = near_copies()
    stage_arrive(4, 0)
    for copy in near_a:
        copy.start()
    arrive(block(pb, z, c, 1))
    for copy in near_b:
        copy.start()
    for s in (0, 1):
        stage_arrive(1, s)

    def plane(j):
        from_sibling(j)
        trace_step(j)

    def step(g, _):
        pl.when(g <= 3)(lambda: ring(2 * g + 1, (2,)))
        pl.when(g <= 2)(lambda: ring(2 * g + 2, (2,)))
        pl.when(jnp.logical_and(g >= 1, g <= 4))(lambda: plane(2 * g - 1))
        pl.when(g == 4)(lambda: hand_back(0, (0, 1)))

        @pl.when(g == 1)
        def _():
            for s in (0, 1):
                stage_arrive(2, s)
                stage_arrive(3, s)
                pltpu.make_async_copy(meta.at[s], meta.at[s], meta_recv.at[s]).wait()
            suffix_self()

        pl.when(jnp.logical_and(g >= 1, g <= 4))(lambda: suffix_step(0, (zstep(2 * g - 2), zstep(2 * g - 1))))
        pl.when(g == 4)(lambda: hand_back(1, (0,)))
        pl.when(g <= 3)(lambda: ring(2 * g + 1, (0, 1)))
        pl.when(g <= 2)(lambda: ring(2 * g + 2, (0, 1)))
        pl.when(g <= 3)(lambda: plane(2 * g))
        pl.when(g <= 3)(lambda: cross(2 * g + 1))
        pl.when(g <= 2)(lambda: cross(2 * g + 2))
        pl.when(g >= 2)(lambda: suffix_step(1, (zstep(2 * g - 4), zstep(2 * g - 3))))
        return 0

    lax.fori_loop(0, 6, step, 0)
    hand_back(1, (1,))

    for kind in range(4):
        stage_drain(kind)
    pl.when(u == 0)(lambda: stage_drain(4))
    for i in (0, 1):
        remote, _, is_self = meta_copy(i)
        if i:
            remote.wait_send()
        else:
            pl.when(jnp.logical_not(is_self))(remote.wait_send)
    for copy in own_copies() + near_a + near_b:
        copy.wait_send()

    def finish(j, _):
        drain(j)
        return 0

    lax.fori_loop(1, 8, finish, 0)
    for kind in (0, 1):
        for s in (0, 1):
            for i in range(4):
                remote, _, is_self = returns(kind, s, i)
                if i:
                    remote.wait_send()
                else:
                    pl.when(jnp.logical_not(is_self))(remote.wait_send)
    pltpu.make_async_copy(tout, tout, o_recv.at[0]).wait()
    pltpu.make_async_copy(sout, sout, o_recv.at[1]).wait()


def settle(a, b, a_out, b_out):
    a_out[...] = a[...]
    b_out[...] = b[...]


def local(trace_q, trace_key_value, suffix_q, suffix_key_value, prefix_len, del_start, del_end):
    any_space = pl.BlockSpec(memory_space=pl.ANY)
    scalar = pl.BlockSpec(memory_space=pltpu.SMEM)
    bf16, f32 = jnp.bfloat16, jnp.float32
    tout, sout = pl.pallas_call(
        kernel,
        out_shape=(
            jax.ShapeDtypeStruct(trace_q.shape, bf16),
            jax.ShapeDtypeStruct(trace_q.shape, bf16),
        ),
        in_specs=[any_space] * 4 + [scalar] * 3,
        out_specs=(any_space, any_space),
        scratch_shapes=[
            pltpu.VMEM((8192, 256), bf16),
            pltpu.VMEM((2, 128, QCOL), bf16),
            pltpu.VMEM((2, 128, QCOL), bf16),
            pltpu.VMEM((2, 128, 256), bf16),
            pltpu.VMEM((2, 128, QCOL), bf16),
            pltpu.VMEM((2, 128, QCOL), bf16),
            pltpu.VMEM((8, 128), jnp.int32),
            pltpu.VMEM((2, 8, 128), jnp.int32),
            pltpu.VMEM((4, ROWS, HEAD), f32),
            pltpu.VMEM((4, ROWS, HEAD), f32),
            pltpu.VMEM((4, ROWS, HEAD), f32),
            pltpu.SemaphoreType.DMA((5, 8)),
            pltpu.SemaphoreType.DMA((5, 2)),
            pltpu.SemaphoreType.DMA((2,)),
            pltpu.SemaphoreType.DMA((2,)),
            pltpu.SemaphoreType.DMA((11,)),
            pltpu.SemaphoreType.DMA((8, 8)),
            pltpu.SemaphoreType.DMA((64,)),
            pltpu.SemaphoreType.DMA((2, 2, 4)),
            pltpu.SemaphoreType.DMA((2,)),
        ],
        compiler_params=pltpu.CompilerParams(
            collective_id=0, has_side_effects=True, vmem_limit_bytes=56 * 2**20
        ),
        cost_estimate=pl.CostEstimate(flops=9 * 10**9, bytes_accessed=4 * 10**6, transcendentals=17 * 10**6),
    )(
        trace_q, trace_key_value, suffix_q[0], suffix_key_value[0], prefix_len, del_start, del_end
    )
    whole = pl.BlockSpec(memory_space=pltpu.VMEM)
    tout, sout = pl.pallas_call(
        settle,
        out_shape=(jax.ShapeDtypeStruct(trace_q.shape, bf16),) * 2,
        in_specs=[whole] * 2,
        out_specs=(whole, whole),
    )(tout, sout)
    return tout, sout[None]


def solution(mesh):
    return jax.shard_map(
        local,
        mesh=mesh,
        in_specs=(
            P(("ctx", "tp"), None),
            P(("ctx", "tp"), None),
            P("ctx", "tp", None),
            P("ctx", "tp", None),
            P("ctx"),
            P("ctx"),
            P("ctx"),
        ),
        out_specs=(P(("ctx", "tp"), None), P("ctx", "tp", None)),
        check_vma=False,
    )
```

```python
import math

import jax
import jax.numpy as jnp
from jax import lax
from jax.experimental import pallas as pl
from jax.experimental.pallas import tpu as pltpu
from jax.sharding import PartitionSpec as P

HEAD = 128
GROUP = 5
ROWS = GROUP * 128
QCOL = GROUP * HEAD
SCALE = HEAD ** (-0.5) * math.log2(math.e)
LOW = -1e30
MESH = pl.DeviceIdType.MESH


def dot(a, b, ca, cb):
    return lax.dot_general(a, b, (((ca,), (cb,)), ((), ())), preferred_element_type=jnp.float32)


def kernel(
    tq, tkv, sq, skv, pre, first, last,
    tout, sout,
    kvb, tqb, sqb, skb, tob, sob, meta_out, meta, acc, m, l,
    st_send, st_recv, meta_send, meta_recv, ag0, ag_send, ag_recv, o_send, o_recv,
):
    ctx = lax.axis_index("ctx")
    tp = lax.axis_index("tp")
    x = ctx // 16
    z = (ctx // 2) % 8
    yh = ctx % 2
    yl = tp // 2
    c = tp % 2
    u = x // 2
    p = ((x + 1) // 2) % 2
    pb = 1 - p
    cb = 1 - c
    head = u * 4 + yh * 2 + yl

    def xof(side, par):
        return par + side * (3 - 2 * par)

    def dev(side, par, zz, yyh, yyl, cc):
        return (xof(side, par) * 16 + zz * 2 + yyh, yyl * 2 + cc)

    def flip(a, by):
        return 1 - a if by else a

    home = (yh + u) % 2
    at_home = c == home
    spot = yl * 2 + c

    up = dev(u, p, (z + 1) % 8, yh, yl, c)
    down = dev(u, p, (z + 7) % 8, yh, yl, c)
    across = dev(u, pb, z, yh, yl, c)
    sibling = dev(u, p, z, yh, yl, cb)

    barrier = pltpu.get_barrier_semaphore()
    for i in range(1, 32):
        pl.semaphore_signal(
            barrier, inc=1, device_id_type=MESH,
            device_id=dev(
                flip(u, i // 8 % 2), flip(p, i // 16), z, flip(yh, i // 4 % 2), flip(yl, i // 2 % 2), flip(c, i % 2)
            ),
        )
    for d in (up, down):
        pl.semaphore_signal(barrier, inc=1, device_id=d, device_id_type=MESH)
    pl.semaphore_wait(barrier, 33)

    def block(par, zz, cc, s):
        xx = par if s == 0 else 3 - par
        return zz * 8 + xx * 2 + (cc + s) % 2

    def rows(b):
        return kvb.at[pl.ds(pl.multiple_of(b * 128, 128), 128), :]

    mine = pl.ds(pl.multiple_of(spot * 32, 32), 32)
    here = pl.ds(pl.multiple_of((z * 8 + x * 2 + yh) * 128 + spot * 32, 32), 32)

    def targets(kind, i):
        h2 = flip(u, i // 4) * 4 + flip(yh, i // 2 % 2) * 2 + flip(yl, i % 2)
        to = dev(flip(u, i // 4), pb if kind == 4 else p, z, flip(yh, i // 2 % 2), flip(yl, i % 2), home)
        wide = pl.ds(pl.multiple_of(h2 * QCOL, 128), QCOL)
        pair = pl.ds(pl.multiple_of(h2 * 256, 128), 256)
        src, dst = (
            (tkv.at[:, pair], kvb.at[here, :]),
            (tq.at[:, wide], tqb.at[u, mine, :]),
            (skv.at[:, pair], skb.at[u, mine, :]),
            (sq.at[:, wide], sqb.at[u, mine, :]),
            (tkv.at[:, pair], kvb.at[here, :]),
        )[kind]
        remote = pltpu.make_async_remote_copy(
            src, dst, st_send.at[kind, i], st_recv.at[kind, u], device_id=to, device_id_type=MESH
        )
        local = pltpu.make_async_copy(src, dst, st_recv.at[kind, u])
        return remote, local

    def stage_start(kind):
        for i in range(7, -1, -1):
            remote, local = targets(kind, i)
            if i or kind == 4:
                remote.start()
            else:
                pl.when(at_home)(local.start)
                pl.when(jnp.logical_not(at_home))(remote.start)

    def stage_drain(kind):
        for i in range(7, -1, -1):
            remote, _ = targets(kind, i)
            if i or kind == 4:
                remote.wait_send()
            else:
                pl.when(jnp.logical_not(at_home))(remote.wait_send)

    def stage_arrive(kind, s):
        dst = (rows(block(p, z, c, s)), tqb.at[s], skb.at[s], sqb.at[s], rows(block(pb, z, c, s)))[kind]
        pltpu.make_async_copy(dst, dst, st_recv.at[kind, s]).wait()

    def meta_copy(i):
        to = dev(flip(u, i), p, z, yl, c, home)
        is_self = jnp.logical_and(jnp.logical_and(yl == yh, c == yl), at_home) if i == 0 else None
        remote = pltpu.make_async_remote_copy(
            meta_out, meta.at[u], meta_send.at[i], meta_recv.at[u], device_id=to, device_id_type=MESH
        )
        local = pltpu.make_async_copy(meta_out, meta.at[u], meta_recv.at[u])
        return remote, local, is_self

    def pass_on(b, to, sem):
        return pltpu.make_async_remote_copy(rows(b), rows(b), sem, ag_recv.at[b], device_id=to, device_id_type=MESH)

    def arrive(b):
        pltpu.make_async_copy(rows(b), rows(b), ag_recv.at[b]).wait()

    def own_copies():
        a, b = block(p, z, c, 0), block(p, z, c, 1)
        return [
            pass_on(b, up, ag0.at[0]),
            pass_on(b, down, ag0.at[1]),
            pass_on(b, across, ag0.at[2]),
            pass_on(a, up, ag0.at[3]),
            pass_on(a, down, ag0.at[4]),
            pass_on(b, sibling, ag0.at[5]),
            pass_on(a, sibling, ag0.at[6]),
        ]

    def near_copies():
        a, b = block(pb, z, c, 0), block(pb, z, c, 1)
        return (
            [pass_on(a, up, ag0.at[7]), pass_on(a, down, ag0.at[8]), pass_on(a, sibling, ag0.at[9])],
            [pass_on(b, sibling, ag0.at[10])],
        )

    def zstep(j):
        return (z + 8 + (1 - 2 * (j % 2)) * ((j + 1) // 2)) % 8

    def ring_copies(j):
        zz = zstep(j)
        step = 2 * (j % 2) - 1
        onward = dev(u, p, (z + 8 + step) % 8, yh, yl, c)
        early = j <= 4
        go = (
            jnp.logical_or(early, j == 5),
            jnp.logical_or(early, j == 6),
            jnp.logical_or(early, j == 5 + c),
        )
        ids = (block(p, zz, c, 0), block(pb, zz, c, 0), block(p, zz, c, 1))
        return zz, go, ids, onward

    def ring(j, which):
        zz, go, ids, onward = ring_copies(j)
        for i in which:
            arrive(ids[i])
            pl.when(go[i])(pass_on(ids[i], onward, ag_send.at[j, i]).start)
            if i == 2:
                pass_on(ids[i], across, ag_send.at[j, 6]).start()
            pass_on(ids[i], sibling, ag_send.at[j, 3 + i]).start()

    def cross(j):
        b = block(pb, zstep(j), c, 1)
        arrive(b)
        pass_on(b, sibling, ag_send.at[j, 7]).start()

    def drain(j):
        zz, go, ids, onward = ring_copies(j)
        for i in range(3):
            pl.when(go[i])(pass_on(ids[i], onward, ag_send.at[j, i]).wait_send)
            pass_on(ids[i], sibling, ag_send.at[j, 3 + i]).wait_send()
        pass_on(ids[2], across, ag_send.at[j, 6]).wait_send()
        pass_on(block(pb, zz, c, 1), sibling, ag_send.at[j, 7]).wait_send()

    def from_sibling(j):
        zz = zstep(j)
        for par in (0, 1):
            for s in (0, 1):
                arrive(block(par, zz, cb, s))

    def queries(buf, s):
        return jnp.concatenate([buf[s, :, i * HEAD:(i + 1) * HEAD] for i in range(GROUP)], axis=0)

    def wide_of(a, n):
        return jnp.concatenate([a] * n, axis=1)

    def fold(q, pieces, r=slice(0, ROWS)):
        before = m[q, r]
        cols = [sc[:, t * 128:(t + 1) * 128] for sc, _ in pieces for t in range(sc.shape[1] // 128)]
        top = cols[0]
        for col in cols[1:]:
            top = jnp.maximum(top, col)
        now = jnp.maximum(before, jnp.max(top, axis=1, keepdims=True) * SCALE)
        m[q, r] = now
        shrink = jnp.exp2(before - now)
        total, part = acc[q, r] * shrink, l[q, r] * shrink
        for sc, v in pieces:
            n = sc.shape[1] // 128
            w = jnp.exp2(sc * SCALE - wide_of(now, n))
            for t in range(n):
                part = part + w[:, t * 128:(t + 1) * 128]
            total = total + dot(w.astype(jnp.bfloat16), v, 1, 0)
        acc[q, r] = total
        l[q, r] = part

    def trace_body(zz, par, reach):
        at = pl.multiple_of(zz * 1024, 1024)
        half = ROWS // 2
        work = []
        for s in (0, 1):
            n = (par if s == 0 else 3 - par) + reach
            if n == 0:
                continue
            q = queries(tqb, s)
            for r in (slice(0, half), slice(half, ROWS)):
                sc = dot(q[r], kvb[pl.ds(at, n * 256), :HEAD], 1, 1)
                if reach:
                    row = (lax.broadcasted_iota(jnp.int32, (half, 256), 0) + r.start) % 128
                    lane = lax.broadcasted_iota(jnp.int32, (half, 256), 1)
                    seen = lane - row <= (z - zz) * 256 + ((c + s) % 2) * 128
                    tail = jnp.where(seen, sc[:, (n - 1) * 256:], LOW)
                    sc = tail if n == 1 else jnp.concatenate([sc[:, :(n - 1) * 256], tail], axis=1)
                work.append((s, sc, n, r))
        for s, sc, n, r in work:
            fold(s, [(sc, kvb[pl.ds(at, n * 256), HEAD:])], r)

    def trace_step(j):
        zz = zstep(j)
        for par in (0, 1):
            for reach in (0, 1):
                fits = jnp.logical_and(p == par, zz <= z if reach else zz > z)
                pl.when(fits)(lambda par=par, reach=reach: trace_body(zz, par, reach))

    def suffix_self():
        for s in (0, 1):
            sc = dot(queries(sqb, s), skb[s, :, :HEAD], 1, 1)
            row = lax.broadcasted_iota(jnp.int32, (ROWS, 128), 0) % 128
            lane = lax.broadcasted_iota(jnp.int32, (ROWS, 128), 1)
            fold(2 + s, [(jnp.where(lane <= row, sc, LOW), skb[s, :, HEAD:])])

    def suffix_step(s, planes):
        q = queries(sqb, s)
        limit, lo, hi = meta[s, 0:1, :], meta[s, 1:2, :], meta[s, 2:3, :]
        biases = []
        for zz in planes:
            bias = []
            for t in range(8):
                pos = (t // 2) * 2048 + (t % 2) * 128 + zz * 256 + lax.broadcasted_iota(jnp.int32, (1, 128), 1)
                seen = jnp.logical_and(pos < limit, jnp.logical_or(pos < lo, pos >= hi))
                bias.append(jnp.where(seen, 0.0, LOW))
            biases.append(jnp.concatenate(bias, axis=1))
        halves = (slice(0, ROWS // 2), slice(ROWS // 2, ROWS))
        places = [pl.ds(pl.multiple_of(zz * 1024, 1024), 1024) for zz in planes]
        scores = [
            [dot(q[r], kvb[at, :HEAD], 1, 1) + bias for at, bias in zip(places, biases)] for r in halves
        ]
        for r, row in zip(halves, scores):
            fold(2 + s, [(sc, kvb[at, HEAD:]) for sc, at in zip(row, places)], r)

    def returns(kind, s, i):
        buf, out = ((tob, tout), (sob, sout))[kind]
        yyl, cc = flip(yl, i // 2), flip(c, i % 2)
        to = dev(s, p, z, (c + s) % 2, yyl, cc)
        part = pl.ds(pl.multiple_of((yyl * 2 + cc) * 32, 32), 32)
        place = pl.ds(pl.multiple_of(head * QCOL, 128), QCOL)
        remote = pltpu.make_async_remote_copy(
            buf.at[s, part, :], out.at[:, place], o_send.at[kind, s, i], o_recv.at[kind],
            device_id=to, device_id_type=MESH,
        )
        local = pltpu.make_async_copy(buf.at[s, part, :], out.at[:, place], o_recv.at[kind])
        is_self = jnp.logical_and(at_home, u == s) if i == 0 else None
        return remote, local, is_self

    def hand_back(kind, slots):
        buf = (tob, sob)[kind]
        for s in slots:
            q = kind * 2 + s
            res = (acc[q] / jnp.sum(l[q], axis=1, keepdims=True)).astype(jnp.bfloat16)
            for i in range(GROUP):
                buf[s, :, i * HEAD:(i + 1) * HEAD] = res[i * 128:(i + 1) * 128]
            for i in range(3, -1, -1):
                remote, local, is_self = returns(kind, s, i)
                if i:
                    remote.start()
                else:
                    pl.when(is_self)(local.start)
                    pl.when(jnp.logical_not(is_self))(remote.start)

    stage_start(0)
    pl.when(u == 0)(lambda: stage_start(4))
    meta_out[0:1, :] = jnp.full((1, 128), pre[0], jnp.int32)
    meta_out[1:2, :] = jnp.full((1, 128), first[0], jnp.int32)
    meta_out[2:8, :] = jnp.full((6, 128), last[0], jnp.int32)
    stage_start(1)
    for i in (0, 1):
        remote, local, is_self = meta_copy(i)
        if i:
            remote.start()
        else:
            pl.when(is_self)(local.start)
            pl.when(jnp.logical_not(is_self))(remote.start)

    acc[...] = jnp.zeros_like(acc)
    l[...] = jnp.zeros_like(l)
    m[...] = jnp.full_like(m, LOW)

    for s in (0, 1):
        stage_arrive(0, s)
    for copy in own_copies():
        copy.start()
    stage_start(3)
    stage_start(2)
    near_a, near_b = near_copies()
    stage_arrive(4, 0)
    for copy in near_a:
        copy.start()
    arrive(block(pb, z, c, 1))
    for copy in near_b:
        copy.start()
    for s in (0, 1):
        stage_arrive(1, s)

    def plane(j):
        from_sibling(j)
        trace_step(j)

    def step(g, _):
        pl.when(g <= 3)(lambda: ring(2 * g + 1, (2,)))
        pl.when(g <= 2)(lambda: ring(2 * g + 2, (2,)))
        pl.when(g <= 4)(lambda: plane(jnp.maximum(2 * g - 1, 0)))
        pl.when(g == 4)(lambda: hand_back(0, (0, 1)))

        pl.when(g <= 3)(lambda: ring(2 * g + 1, (0,)))
        pl.when(g <= 2)(lambda: ring(2 * g + 2, (0,)))

        @pl.when(g == 1)
        def _():
            for s in (0, 1):
                stage_arrive(2, s)
                stage_arrive(3, s)
                pltpu.make_async_copy(meta.at[s], meta.at[s], meta_recv.at[s]).wait()
            suffix_self()

        pl.when(jnp.logical_and(g >= 1, g <= 4))(lambda: suffix_step(0, (zstep(2 * g - 2), zstep(2 * g - 1))))
        pl.when(g == 4)(lambda: hand_back(1, (0,)))
        pl.when(g <= 3)(lambda: ring(2 * g + 1, (1,)))
        pl.when(g <= 2)(lambda: ring(2 * g + 2, (1,)))
        pl.when(jnp.logical_and(g >= 1, g <= 3))(lambda: plane(2 * g))
        pl.when(g <= 3)(lambda: cross(2 * g + 1))
        pl.when(g <= 2)(lambda: cross(2 * g + 2))
        pl.when(g >= 1)(lambda: suffix_step(1, (zstep(2 * g - 2), zstep(2 * g - 1))))
        return 0

    lax.fori_loop(0, 5, step, 0)
    hand_back(1, (1,))

    for kind in range(4):
        stage_drain(kind)
    pl.when(u == 0)(lambda: stage_drain(4))
    for i in (0, 1):
        remote, _, is_self = meta_copy(i)
        if i:
            remote.wait_send()
        else:
            pl.when(jnp.logical_not(is_self))(remote.wait_send)
    for copy in own_copies() + near_a + near_b:
        copy.wait_send()

    def finish(j, _):
        drain(j)
        return 0

    lax.fori_loop(1, 8, finish, 0)
    for kind in (0, 1):
        for s in (0, 1):
            for i in range(4):
                remote, _, is_self = returns(kind, s, i)
                if i:
                    remote.wait_send()
                else:
                    pl.when(jnp.logical_not(is_self))(remote.wait_send)
    pltpu.make_async_copy(tout, tout, o_recv.at[0]).wait()
    pltpu.make_async_copy(sout, sout, o_recv.at[1]).wait()


def settle(a, b, a_out, b_out, a_here, b_here, sems):
    pairs = ((a, a_here, a_out), (b, b_here, b_out))
    reads = [pltpu.make_async_copy(src, via, sems.at[i]) for i, (src, via, _) in enumerate(pairs)]
    writes = [pltpu.make_async_copy(via, dst, sems.at[2 + i]) for i, (_, via, dst) in enumerate(pairs)]
    for copy in reads:
        copy.start()
    for read, write in zip(reads, writes):
        read.wait()
        write.start()
    for copy in writes:
        copy.wait()


def local(trace_q, trace_key_value, suffix_q, suffix_key_value, prefix_len, del_start, del_end):
    any_space = pl.BlockSpec(memory_space=pl.ANY)
    scalar = pl.BlockSpec(memory_space=pltpu.SMEM)
    bf16, f32 = jnp.bfloat16, jnp.float32
    tout, sout = pl.pallas_call(
        kernel,
        out_shape=(
            jax.ShapeDtypeStruct(trace_q.shape, bf16),
            jax.ShapeDtypeStruct(trace_q.shape, bf16),
        ),
        in_specs=[any_space] * 4 + [scalar] * 3,
        out_specs=(any_space, any_space),
        scratch_shapes=[
            pltpu.VMEM((8192, 256), bf16),
            pltpu.VMEM((2, 128, QCOL), bf16),
            pltpu.VMEM((2, 128, QCOL), bf16),
            pltpu.VMEM((2, 128, 256), bf16),
            pltpu.VMEM((2, 128, QCOL), bf16),
            pltpu.VMEM((2, 128, QCOL), bf16),
            pltpu.VMEM((8, 128), jnp.int32),
            pltpu.VMEM((2, 8, 128), jnp.int32),
            pltpu.VMEM((4, ROWS, HEAD), f32),
            pltpu.VMEM((4, ROWS, HEAD), f32),
            pltpu.VMEM((4, ROWS, HEAD), f32),
            pltpu.SemaphoreType.DMA((5, 8)),
            pltpu.SemaphoreType.DMA((5, 2)),
            pltpu.SemaphoreType.DMA((2,)),
            pltpu.SemaphoreType.DMA((2,)),
            pltpu.SemaphoreType.DMA((11,)),
            pltpu.SemaphoreType.DMA((8, 8)),
            pltpu.SemaphoreType.DMA((64,)),
            pltpu.SemaphoreType.DMA((2, 2, 4)),
            pltpu.SemaphoreType.DMA((2,)),
        ],
        compiler_params=pltpu.CompilerParams(
            collective_id=0, has_side_effects=True, vmem_limit_bytes=56 * 2**20
        ),
        cost_estimate=pl.CostEstimate(flops=9 * 10**9, bytes_accessed=4 * 10**6, transcendentals=17 * 10**6),
    )(
        trace_q, trace_key_value, suffix_q[0], suffix_key_value[0], prefix_len, del_start, del_end
    )
    tout, sout = pl.pallas_call(
        settle,
        out_shape=(jax.ShapeDtypeStruct(trace_q.shape, bf16),) * 2,
        in_specs=[any_space] * 2,
        out_specs=(any_space, any_space),
        scratch_shapes=[pltpu.VMEM(trace_q.shape, bf16)] * 2 + [pltpu.SemaphoreType.DMA((4,))],
    )(tout, sout)
    return tout, sout[None]


def solution(mesh):
    return jax.shard_map(
        local,
        mesh=mesh,
        in_specs=(
            P(("ctx", "tp"), None),
            P(("ctx", "tp"), None),
            P("ctx", "tp", None),
            P("ctx", "tp", None),
            P("ctx"),
            P("ctx"),
            P("ctx"),
        ),
        out_specs=(P(("ctx", "tp"), None), P("ctx", "tp", None)),
        check_vma=False,
    )
```
